32 devices in a mesh: dp: 4 (over z), tensor: 8 (over y, x, core).
Axes of the slice: x: 2, y: 2, z: 4, core: 2. Of those that a mesh axis runs over, the one named last changes fastest.
Arguments:
- queries: bfloat16 [4096, 2048], P(('dp', 'tensor'))
- key_rows: bfloat16 [4096, 1024], P(('dp', 'tensor'))
- value_rows: bfloat16 [4096, 1024], P(('dp', 'tensor')), may hold values from -6 to 6
- out_grad: bfloat16 [4096, 2048], P(('dp', 'tensor')), may hold values from -6 to 6
Outputs:
- attended: bfloat16 [4096, 2048], P(('dp', 'tensor'))
- grad_queries: bfloat16 [4096, 2048], P(('dp', 'tensor'))
- grad_keys: bfloat16 [4096, 1024], P(('dp', 'tensor'))
- grad_values: bfloat16 [4096, 1024], P(('dp', 'tensor'))
The draws below stay inside these ranges and needn't reach their ends.
All inputs are finite; a program needn't handle non-finite values.
Results may differ from the reference program's by a relative error of at most 0.0075.
Values may be sent and summed in bfloat16 or wider, within the bound.
A program may use at most 64 MiB of HBM per device.

```python
import math
import jax
import jax.numpy as jnp
from jax import lax

HEADS = 16
KV_HEADS = 8
HEAD_DIM = 128
WINDOW = 1024
QUERY_SCALE = 168
TOK_DEV = 128
TOKENS = 4096


def key_parts(base_key):
    folded_key = jax.random.fold_in(base_key, 7)
    unit_key, scale_key = jax.random.split(folded_key)
    shape = (TOKENS, KV_HEADS * HEAD_DIM)
    units = jax.random.truncated_normal(unit_key, -4.0, 4.0, shape, jnp.float32)
    scales = jnp.exp(jax.random.uniform(scale_key, (TOKENS, 1), jnp.float32, math.log(0.5), math.log(2.0)))
    return (units, scales)


def draw_key_rows(key, part):
    units, scales = key_parts(key)
    keys_out = units * scales
    return keys_out.astype(jnp.bfloat16)


def draw_queries(key, part):
    query_key = jax.random.fold_in(key, 13)
    value_key, spread_key = jax.random.split(query_key)
    shape = (TOKENS, HEADS * HEAD_DIM)
    drawn = jax.random.truncated_normal(value_key, -4.0, 4.0, shape, jnp.float32)
    spread = jnp.exp(jax.random.uniform(spread_key, (TOKENS, 1), jnp.float32, math.log(0.5), math.log(2.0)))
    result = drawn * spread
    return result.astype(jnp.bfloat16)


def steps_of(stream_key, dims, pieces, low, top_value):
    def one(axis_at, shards_of):
        steps = jax.random.uniform(jax.random.fold_in(jax.random.fold_in(stream_key, 6), axis_at), (shards_of,), jnp.float32, low / len(pieces), top_value / len(pieces))
        return jnp.repeat(jnp.exp(steps), dims[axis_at] // shards_of).reshape((-1,) + (1,) * (len(dims) - axis_at - 1))

    gain = one(*pieces[0])
    for cut in pieces[1:]:
        gain = gain * one(*cut)
    return gain


def scatter_about(key, dims, deviation, most, pieces=(), kind=jnp.bfloat16):
    factor_of = steps_of(key, dims, pieces, -0.22, 0.18) if pieces else 1.0
    values = jax.random.normal(key, dims, jnp.float32) * deviation * factor_of
    return jnp.minimum(jnp.maximum(values, -most), most).astype(kind)


def setup_inputs(seed: int = 0) -> dict:
    streams_of = jax.random.split(jax.random.key(seed), 5)
    queries = draw_queries(jax.random.fold_in(streams_of[4], 71), 0)
    key_rows = draw_key_rows(jax.random.fold_in(streams_of[4], 71), 0)
    value_rows = scatter_about(streams_of[2], (TOKENS, KV_HEADS * HEAD_DIM), 1.0, 6.0, ((0, 32),))
    out_grad = scatter_about(streams_of[3], (TOKENS, HEADS * HEAD_DIM), 1.0, 6.0, ((0, 32),))
    return {"queries": queries, "key_rows": key_rows, "value_rows": value_rows, "out_grad": out_grad}


masked_score = -1.0e30


def low_round(values):
    return lax.optimization_barrier(values.astype(jnp.bfloat16)).astype(jnp.float32)


def reference(queries, key_rows, value_rows, out_grad):
    repeat_count = HEADS // KV_HEADS
    span_rows = WINDOW + TOK_DEV
    block_count = TOKENS // TOK_DEV
    score_scale = QUERY_SCALE ** -0.5
    padding = jnp.zeros((WINDOW, KV_HEADS * HEAD_DIM), key_rows.dtype)
    keys_padded = jnp.concatenate([padding, key_rows], axis=0)
    values_padded = jnp.concatenate([padding, value_rows], axis=0)

    def block_step(carry, block_index):
        total_keys, total_values = carry
        first_row = block_index * TOK_DEV
        query_block = lax.dynamic_slice_in_dim(queries, first_row, TOK_DEV, 0).astype(jnp.float32).reshape(TOK_DEV, KV_HEADS, repeat_count, HEAD_DIM)
        grad_block = lax.dynamic_slice_in_dim(out_grad, first_row, TOK_DEV, 0).astype(jnp.float32).reshape(TOK_DEV, KV_HEADS, repeat_count, HEAD_DIM)
        key_block = lax.dynamic_slice_in_dim(keys_padded, first_row, span_rows, 0).astype(jnp.float32).reshape(span_rows, KV_HEADS, HEAD_DIM)
        value_block = lax.dynamic_slice_in_dim(values_padded, first_row, span_rows, 0).astype(jnp.float32).reshape(span_rows, KV_HEADS, HEAD_DIM)
        query_pos = first_row + lax.broadcasted_iota(jnp.int32, (TOK_DEV, span_rows), 0)
        key_pos = first_row - WINDOW + lax.broadcasted_iota(jnp.int32, (TOK_DEV, span_rows), 1)
        allowed = (key_pos <= query_pos) & (key_pos > query_pos - WINDOW) & (key_pos >= 0)
        scores = score_scale * jnp.einsum("igrd,jgd->grij", query_block, key_block)
        scores = jnp.where(allowed[None, None], scores, masked_score)
        peak = jnp.max(scores, axis=-1, keepdims=True)
        expo = jnp.exp(scores - peak)
        probs = expo / jnp.sum(expo, axis=-1, keepdims=True)
        probs_low = low_round(probs)
        out_full = jnp.einsum("grij,jgd->igrd", probs_low, value_block)
        grad_probs = jnp.einsum("igrd,jgd->grij", grad_block, value_block)
        delta = jnp.transpose(jnp.sum(grad_block * out_full, axis=-1), (1, 2, 0))
        grad_scores = low_round(score_scale * probs * (grad_probs - delta[..., None]))
        grad_query = jnp.einsum("grij,jgd->igrd", grad_scores, key_block)
        key_term = low_round(jnp.einsum("grij,igrd->jgd", grad_scores, query_block))
        value_term = low_round(jnp.einsum("grij,igrd->jgd", probs_low, grad_block))
        old_keys = lax.dynamic_slice_in_dim(total_keys, first_row, span_rows, 0)
        old_values = lax.dynamic_slice_in_dim(total_values, first_row, span_rows, 0)
        total_keys = lax.dynamic_update_slice_in_dim(total_keys, old_keys + key_term.reshape(span_rows, KV_HEADS * HEAD_DIM), first_row, 0)
        total_values = lax.dynamic_update_slice_in_dim(total_values, old_values + value_term.reshape(span_rows, KV_HEADS * HEAD_DIM), first_row, 0)
        out_rows = out_full.astype(jnp.bfloat16).reshape(TOK_DEV, HEADS * HEAD_DIM)
        grad_rows = grad_query.astype(jnp.bfloat16).reshape(TOK_DEV, HEADS * HEAD_DIM)
        return (total_keys, total_values), (out_rows, grad_rows)

    start_sums = jnp.zeros((WINDOW + TOKENS, KV_HEADS * HEAD_DIM), jnp.float32)
    sums, stacked = lax.scan(block_step, (start_sums, start_sums), jnp.arange(block_count, dtype=jnp.int32))
    attended = stacked[0].reshape(TOKENS, HEADS * HEAD_DIM)
    grad_queries = stacked[1].reshape(TOKENS, HEADS * HEAD_DIM)
    grad_keys = sums[0][WINDOW:].astype(jnp.bfloat16)
    grad_values = sums[1][WINDOW:].astype(jnp.bfloat16)
    return (attended, grad_queries, grad_keys, grad_values)
```

```python
import functools

import jax
import jax.numpy as jnp
from jax import lax
from jax.experimental import pallas as pl
from jax.experimental.pallas import tpu as pltpu
from jax.sharding import PartitionSpec as P

HEAD_DIM = 128
WINDOW = 1024
QUERY_SCALE = 168
LOG2E = 1.4426950408889634

masked_score = -1e30
MESH = pl.DeviceIdType.MESH


def contract(left, right, dims):
    return lax.dot_general(left, right, (dims, ((), ())), preferred_element_type=jnp.float32)


def kernel(
    team, repeat, tensor_size, total,
    q_hbm, k_hbm, v_hbm, g_hbm,
    att_hbm, gq_hbm, gk_hbm, gv_hbm,
    qb, gb, kv, kvt, dk, dv, att, gq, back, later, fin, land, work, pbuf, dbuf,
    in_send, in_recv, fwd_send, fwd_recv, out_send, out_recv,
    back_send, back_recv, fin_send, fin_recv, store_sem,
):
    rows = q_hbm.shape[0]
    width = repeat * HEAD_DIM
    scale = QUERY_SCALE ** (-0.5)
    me = lax.axis_index("dp") * tensor_size + lax.axis_index("tensor")
    member = lax.rem(me, team)
    base = me - member
    has_prev = me >= team
    has_next = me + team < total

    def place(index):
        return (lax.div(index, tensor_size), lax.rem(index, tensor_size))

    def peer(step):
        return lax.rem(member + step, team)

    barrier = pltpu.get_barrier_semaphore()
    for step in range(1, team):
        pl.semaphore_signal(barrier, inc=1, device_id=place(base + peer(step)), device_id_type=MESH)

    @pl.when(has_prev)
    def _():
        pl.semaphore_signal(barrier, inc=1, device_id=place(me - team), device_id_type=MESH)

    @pl.when(has_next)
    def _():
        pl.semaphore_signal(barrier, inc=1, device_id=place(me + team), device_id_type=MESH)

    pl.semaphore_wait(barrier, team - 1 + has_prev.astype(jnp.int32) + has_next.astype(jnp.int32))

    def wide(index):
        return pl.ds(pl.multiple_of(index * width, width), width)

    def narrow(index):
        return pl.ds(pl.multiple_of(index * HEAD_DIM, HEAD_DIM), HEAD_DIM)

    k_half = pl.ds(0, HEAD_DIM)
    v_half = pl.ds(HEAD_DIM, HEAD_DIM)

    def pieces(to, slot):
        return (
            (k_hbm.at[:, narrow(to)], kv.at[team + slot, :, k_half]),
            (v_hbm.at[:, narrow(to)], kv.at[team + slot, :, v_half]),
            (q_hbm.at[:, wide(to)], qb.at[slot]),
            (g_hbm.at[:, wide(to)], gb.at[slot]),
        )

    def in_copy(kind, to):
        src, dst = pieces(to, member)[kind]
        return pltpu.make_async_remote_copy(
            src_ref=src, dst_ref=dst,
            send_sem=in_send.at[kind, to], recv_sem=in_recv.at[kind, member],
            device_id=place(base + to), device_id_type=MESH,
        )

    def in_wait(kind, source):
        src, dst = pieces(member, source)[kind]
        pltpu.make_async_copy(src, dst, in_recv.at[kind, source]).wait()

    for kind in range(4):
        src, dst = pieces(member, member)[kind]
        pltpu.make_async_copy(src, dst, in_recv.at[kind, member]).start()
    for kinds in ((0, 1), (2, 3)):
        for step in range(1, team):
            for kind in kinds:
                in_copy(kind, peer(step)).start()

    dk[...] = jnp.zeros_like(dk)
    dv[...] = jnp.zeros_like(dv)

    def fwd_copy(slot):
        return pltpu.make_async_remote_copy(
            src_ref=kv.at[team + slot], dst_ref=kv.at[slot],
            send_sem=fwd_send.at[slot], recv_sem=fwd_recv.at[slot],
            device_id=place(me + team), device_id_type=MESH,
        )

    for step in range(team):
        source = peer(step)
        in_wait(0, source)
        in_wait(1, source)

        @pl.when(has_next)
        def _():
            fwd_copy(source).start()

    def turn(slot):
        kvt[:, pl.ds(pl.multiple_of(slot * rows, rows), rows)] = kv[slot].T

    @pl.loop(0, team)
    def _(slot):
        turn(team + slot)

    @pl.when(jnp.logical_not(has_prev))
    def _():
        kv[pl.ds(0, team)] = jnp.zeros((team,) + kv.shape[1:], kv.dtype)

    @pl.loop(0, team)
    def _(step):
        slot = peer(step)

        @pl.when(has_prev)
        def _():
            pltpu.make_async_copy(kv.at[team + slot], kv.at[slot], fwd_recv.at[slot]).wait()

        turn(slot)

    span = (team + 1) * rows
    key_at = lax.broadcasted_iota(jnp.int32, (rows, repeat * rows), 0)
    query_at = lax.rem(lax.broadcasted_iota(jnp.int32, (rows, repeat * rows), 1), rows)
    factor = scale * LOG2E

    def stack(block):
        return jnp.concatenate(
            [block[:, h * HEAD_DIM : (h + 1) * HEAD_DIM] for h in range(repeat)], axis=0
        )

    def unstack(block):
        return jnp.concatenate([block[h * rows : (h + 1) * rows] for h in range(repeat)], axis=1)

    def out_copy(kind, to):
        buf, ref = ((att, att_hbm), (gq, gq_hbm))[kind]
        return pltpu.make_async_remote_copy(
            src_ref=buf.at[to], dst_ref=ref.at[:, wide(member)],
            send_sem=out_send.at[kind, to], recv_sem=out_recv.at[kind, member],
            device_id=place(base + to), device_id_type=MESH,
        )

    def out_own(kind):
        buf, ref = ((att, att_hbm), (gq, gq_hbm))[kind]
        return pltpu.make_async_copy(
            buf.at[member], ref.at[:, wide(member)], out_recv.at[kind, member]
        )

    def ship(kind, to):
        @pl.when(to != member)
        def _():
            out_copy(kind, to).start()

        @pl.when(to == member)
        def _():
            out_own(kind).start()

    @pl.loop(0, team)
    def _(step):
        b = peer(step)
        in_wait(2, b)
        in_wait(3, b)
        q2 = stack(qb[b])
        g2 = stack(gb[b])
        q2t = q2.T
        g2t = g2.T
        cols = pl.ds(pl.multiple_of(b * rows, rows), span)
        gone = [jnp.logical_and(jnp.logical_not(has_prev), b + r < team) for r in range(team)]
        gone.append(None)
        peak = None
        for r in range(team + 1):
            part = contract(kv[b + r, :, :HEAD_DIM], q2t, ((1,), (0,)))
            if r == 0:
                part = jnp.where(key_at > query_at, part, masked_score)
            if r == team:
                part = jnp.where(key_at <= query_at, part, masked_score)
            work[r] = part
            top = jnp.max(part.reshape(rows // 8, 8, width), axis=0)
            if r < team:
                top = jnp.where(gone[r], masked_score, top)
            peak = top if peak is None else jnp.maximum(peak, top)
        low = jnp.max(peak, axis=0, keepdims=True) * factor
        denom = None
        for r in range(team + 1):
            shift = low if r == team else jnp.where(gone[r], -masked_score, low)
            expo = jnp.exp2(work[r] * factor - shift)
            work[r] = expo
            part = jnp.sum(expo.reshape(rows // 8, 8, width), axis=0)
            denom = part if denom is None else denom + part
        inverse = 1.0 / jnp.sum(denom, axis=0, keepdims=True)
        for r in range(team + 1):
            probs = work[r] * inverse
            work[r] = probs
            pbuf[r * rows : (r + 1) * rows] = probs.astype(jnp.bfloat16)
        out_t = contract(kvt[HEAD_DIM:, cols], pbuf[...], ((1,), (0,)))
        att[b] = unstack(out_t.T).astype(jnp.bfloat16)
        ship(0, b)
        delta = jnp.sum(g2t.astype(jnp.float32) * out_t, axis=0, keepdims=True)
        for r in range(team + 1):
            grad_probs = contract(kv[b + r, :, HEAD_DIM:], g2t, ((1,), (0,)))
            dbuf[r * rows : (r + 1) * rows] = (work[r] * (grad_probs - delta)).astype(jnp.bfloat16)
        dq_t = contract(kvt[:HEAD_DIM, cols], dbuf[...], ((1,), (0,))) * scale
        gq[b] = unstack(dq_t.T).astype(jnp.bfloat16)
        ship(1, b)
        dk[cols, :] += contract(dbuf[...], q2, ((1,), (0,)))
        dv[cols, :] += contract(pbuf[...], g2, ((1,), (0,)))

    def back_copy(slot):
        return pltpu.make_async_remote_copy(
            src_ref=back.at[slot], dst_ref=later.at[slot],
            send_sem=back_send.at[slot], recv_sem=back_recv.at[slot],
            device_id=place(me - team), device_id_type=MESH,
        )

    def sums(slot):
        at = pl.ds(pl.multiple_of(slot * rows, rows), rows)
        return jnp.concatenate([dk[at, :] * scale, dv[at, :]], axis=1)

    @pl.when(has_prev)
    def _():
        @pl.loop(0, team)
        def _(step):
            slot = peer(step)
            back[slot] = sums(slot).astype(jnp.bfloat16)
            back_copy(slot).start()

    def fin_copy(to):
        return pltpu.make_async_remote_copy(
            src_ref=fin.at[to], dst_ref=land.at[member],
            send_sem=fin_send.at[to], recv_sem=fin_recv.at[member],
            device_id=place(base + to), device_id_type=MESH,
        )

    def fin_own():
        return pltpu.make_async_copy(fin.at[member], land.at[member], fin_recv.at[member])

    @pl.when(jnp.logical_not(has_next))
    def _():
        later[...] = jnp.zeros_like(later)

    @pl.loop(0, team)
    def _(step):
        slot = peer(step)

        @pl.when(has_next)
        def _():
            pltpu.make_async_copy(back.at[slot], later.at[slot], back_recv.at[slot]).wait()

        fin[slot] = (sums(team + slot) + later[slot].astype(jnp.float32)).astype(jnp.bfloat16)

        @pl.when(slot != member)
        def _():
            fin_copy(slot).start()

        @pl.when(slot == member)
        def _():
            fin_own().start()

    for step in range(team):
        source = lax.rem(member + team - step, team)
        pltpu.make_async_copy(fin.at[source], land.at[source], fin_recv.at[source]).wait()
        gk = pltpu.make_async_copy(
            land.at[source, :, k_half], gk_hbm.at[:, narrow(source)], store_sem.at[0, source]
        )
        gv = pltpu.make_async_copy(
            land.at[source, :, v_half], gv_hbm.at[:, narrow(source)], store_sem.at[1, source]
        )
        gk.start()
        gv.start()

    for step in range(team):
        source = peer(step)
        for kind in range(2):
            buf, ref = ((att, att_hbm), (gq, gq_hbm))[kind]
            pltpu.make_async_copy(
                buf.at[source], ref.at[:, wide(source)], out_recv.at[kind, source]
            ).wait()
        pltpu.make_async_copy(
            land.at[source, :, k_half], gk_hbm.at[:, narrow(source)], store_sem.at[0, source]
        ).wait()
        pltpu.make_async_copy(
            land.at[source, :, v_half], gv_hbm.at[:, narrow(source)], store_sem.at[1, source]
        ).wait()
    for step in range(1, team):
        to = peer(step)
        for kind in range(4):
            in_copy(kind, to).wait_send()
        for kind in range(2):
            out_copy(kind, to).wait_send()
        fin_copy(to).wait_send()

    @pl.when(has_next)
    def _():
        for slot in range(team):
            fwd_copy(slot).wait_send()

    @pl.when(has_prev)
    def _():
        for slot in range(team):
            back_copy(slot).wait_send()


def local(tensor_size, total, queries, key_rows, value_rows, out_grad):
    rows = queries.shape[0]
    team = WINDOW // rows
    repeat = queries.shape[1] // key_rows.shape[1]
    width = repeat * HEAD_DIM
    assert key_rows.shape[1] == team * HEAD_DIM
    bf16, f32 = jnp.bfloat16, jnp.float32
    dma = pltpu.SemaphoreType.DMA
    pairs = team * (team + 1) * rows * rows * repeat
    return pl.pallas_call(
        functools.partial(kernel, team, repeat, tensor_size, total),
        out_shape=tuple(
            jax.ShapeDtypeStruct(a.shape, bf16) for a in (queries, queries, key_rows, value_rows)
        ),
        in_specs=[pl.BlockSpec(memory_space=pl.ANY)] * 4,
        out_specs=(pl.BlockSpec(memory_space=pl.ANY),) * 4,
        scratch_shapes=[
            pltpu.VMEM((team, rows, width), bf16),
            pltpu.VMEM((team, rows, width), bf16),
            pltpu.VMEM((2 * team, rows, 2 * HEAD_DIM), bf16),
            pltpu.VMEM((2 * HEAD_DIM, 2 * team * rows), bf16),
            pltpu.VMEM((2 * team * rows, HEAD_DIM), f32),
            pltpu.VMEM((2 * team * rows, HEAD_DIM), f32),
            pltpu.VMEM((team, rows, width), bf16),
            pltpu.VMEM((team, rows, width), bf16),
            pltpu.VMEM((team, rows, 2 * HEAD_DIM), bf16),
            pltpu.VMEM((team, rows, 2 * HEAD_DIM), bf16),
            pltpu.VMEM((team, rows, 2 * HEAD_DIM), bf16),
            pltpu.VMEM((team, rows, 2 * HEAD_DIM), bf16),
            pltpu.VMEM((team + 1, rows, width), f32),
            pltpu.VMEM(((team + 1) * rows, width), bf16),
            pltpu.VMEM(((team + 1) * rows, width), bf16),
            dma((4, team)), dma((4, team)),
            dma((team,)), dma((team,)),
            dma((2, team)), dma((2, team)),
            dma((team,)), dma((team,)),
            dma((team,)), dma((team,)),
            dma((2, team)),
        ],
        compiler_params=pltpu.CompilerParams(
            collective_id=0, has_side_effects=True, vmem_limit_bytes=48 * 1024 * 1024
        ),
        cost_estimate=pl.CostEstimate(
            flops=12 * pairs * HEAD_DIM, bytes_accessed=12 * queries.size, transcendentals=pairs
        ),
    )(queries, key_rows, value_rows, out_grad)


def solution(mesh):
    spec = P(("dp", "tensor"), None)
    tensor_size = mesh.shape["tensor"]
    total = mesh.shape["dp"] * tensor_size
    return jax.shard_map(
        functools.partial(local, tensor_size, total),
        mesh=mesh, in_specs=(spec,) * 4, out_specs=(spec,) * 4, check_vma=False,
    )
```

```python
import functools

import jax
import jax.numpy as jnp
from jax import lax
from jax.experimental import pallas as pl
from jax.experimental.pallas import tpu as pltpu
from jax.sharding import PartitionSpec as P

HEAD_DIM = 128
WINDOW = 1024
QUERY_SCALE = 168
LOG2E = 1.4426950408889634

masked_score = -1e30
MESH = pl.DeviceIdType.MESH


def contract(left, right, dims):
    return lax.dot_general(left, right, (dims, ((), ())), preferred_element_type=jnp.float32)


def kernel(
    team, repeat, tensor_size, total,
    q_hbm, k_hbm, v_hbm, g_hbm,
    att_hbm, gq_hbm, gk_hbm, gv_hbm,
    qb, gb, kv, kvt, dk, dv, att, gq, back, later, fin, land, work, pbuf, dbuf,
    in_send, in_recv, fwd_send, fwd_recv, out_send, out_recv,
    back_send, back_recv, fin_send, fin_recv, store_sem,
):
    rows = q_hbm.shape[0]
    width = repeat * HEAD_DIM
    scale = QUERY_SCALE ** (-0.5)
    me = lax.axis_index("dp") * tensor_size + lax.axis_index("tensor")
    member = lax.rem(me, team)
    base = me - member
    has_prev = me >= team
    has_next = me + team < total

    def place(index):
        return (lax.div(index, tensor_size), lax.rem(index, tensor_size))

    def peer(step):
        return lax.rem(member + step, team)

    barrier = pltpu.get_barrier_semaphore()
    for step in range(1, team):
        pl.semaphore_signal(barrier, inc=1, device_id=place(base + peer(step)), device_id_type=MESH)

    @pl.when(has_prev)
    def _():
        pl.semaphore_signal(barrier, inc=1, device_id=place(me - team), device_id_type=MESH)

    @pl.when(has_next)
    def _():
        pl.semaphore_signal(barrier, inc=1, device_id=place(me + team), device_id_type=MESH)

    pl.semaphore_wait(barrier, team - 1 + has_prev.astype(jnp.int32) + has_next.astype(jnp.int32))

    def wide(index):
        return pl.ds(pl.multiple_of(index * width, width), width)

    def narrow(index):
        return pl.ds(pl.multiple_of(index * HEAD_DIM, HEAD_DIM), HEAD_DIM)

    k_half = pl.ds(0, HEAD_DIM)
    v_half = pl.ds(HEAD_DIM, HEAD_DIM)

    def pieces(to, slot):
        return (
            (k_hbm.at[:, narrow(to)], kv.at[team + slot, :, k_half]),
            (v_hbm.at[:, narrow(to)], kv.at[team + slot, :, v_half]),
            (q_hbm.at[:, wide(to)], qb.at[slot]),
            (g_hbm.at[:, wide(to)], gb.at[slot]),
        )

    def in_copy(kind, to):
        src, dst = pieces(to, member)[kind]
        return pltpu.make_async_remote_copy(
            src_ref=src, dst_ref=dst,
            send_sem=in_send.at[kind, to], recv_sem=in_recv.at[kind, member],
            device_id=place(base + to), device_id_type=MESH,
        )

    def in_wait(kind, source):
        src, dst = pieces(member, source)[kind]
        pltpu.make_async_copy(src, dst, in_recv.at[kind, source]).wait()

    for kind in range(4):
        src, dst = pieces(member, member)[kind]
        pltpu.make_async_copy(src, dst, in_recv.at[kind, member]).start()
    for kinds in ((0, 1), (2, 3)):
        for step in range(1, team):
            for kind in kinds:
                in_copy(kind, peer(step)).start()

    dk[...] = jnp.zeros_like(dk)
    dv[...] = jnp.zeros_like(dv)

    def fwd_copy(slot):
        return pltpu.make_async_remote_copy(
            src_ref=kv.at[team + slot], dst_ref=kv.at[slot],
            send_sem=fwd_send.at[slot], recv_sem=fwd_recv.at[slot],
            device_id=place(me + team), device_id_type=MESH,
        )

    for step in range(team):
        source = peer(step)
        in_wait(0, source)
        in_wait(1, source)

        @pl.when(has_next)
        def _():
            fwd_copy(source).start()

    def turn(slot):
        kvt[:, pl.ds(pl.multiple_of(slot * rows, rows), rows)] = kv[slot].T

    @pl.loop(0, team)
    def _(slot):
        turn(team + slot)

    @pl.when(jnp.logical_not(has_prev))
    def _():
        kv[pl.ds(0, team)] = jnp.zeros((team,) + kv.shape[1:], kv.dtype)

    @pl.loop(0, team)
    def _(step):
        slot = peer(step)

        @pl.when(has_prev)
        def _():
            pltpu.make_async_copy(kv.at[team + slot], kv.at[slot], fwd_recv.at[slot]).wait()

        turn(slot)

    span = (team + 1) * rows
    key_at = lax.broadcasted_iota(jnp.int32, (rows, repeat * rows), 0)
    query_at = lax.rem(lax.broadcasted_iota(jnp.int32, (rows, repeat * rows), 1), rows)
    factor = scale * LOG2E

    def stack(block):
        return jnp.concatenate(
            [block[:, h * HEAD_DIM : (h + 1) * HEAD_DIM] for h in range(repeat)], axis=0
        )

    def unstack(block):
        return jnp.concatenate([block[h * rows : (h + 1) * rows] for h in range(repeat)], axis=1)

    def out_copy(kind, to):
        buf, ref = ((att, att_hbm), (gq, gq_hbm))[kind]
        return pltpu.make_async_remote_copy(
            src_ref=buf.at[to], dst_ref=ref.at[:, wide(member)],
            send_sem=out_send.at[kind, to], recv_sem=out_recv.at[kind, member],
            device_id=place(base + to), device_id_type=MESH,
        )

    def out_own(kind):
        buf, ref = ((att, att_hbm), (gq, gq_hbm))[kind]
        return pltpu.make_async_copy(
            buf.at[member], ref.at[:, wide(member)], out_recv.at[kind, member]
        )

    def ship(kind, to):
        @pl.when(to != member)
        def _():
            out_copy(kind, to).start()

        @pl.when(to == member)
        def _():
            out_own(kind).start()

    @pl.loop(0, team)
    def _(step):
        b = peer(step)
        in_wait(2, b)
        in_wait(3, b)
        q2 = stack(qb[b])
        g2 = stack(gb[b])
        q2t = q2.T
        g2t = g2.T
        cols = pl.ds(pl.multiple_of(b * rows, rows), span)
        gone = [jnp.logical_and(jnp.logical_not(has_prev), b + r < team) for r in range(team)]
        gone.append(None)
        peak = None
        for r in range(team + 1):
            part = contract(kv[b + r, :, :HEAD_DIM], q2t, ((1,), (0,)))
            if r == 0:
                part = jnp.where(key_at > query_at, part, masked_score)
            if r == team:
                part = jnp.where(key_at <= query_at, part, masked_score)
            work[r] = part
            top = jnp.max(part.reshape(rows // 8, 8, width), axis=0)
            if r < team:
                top = jnp.where(gone[r], masked_score, top)
            peak = top if peak is None else jnp.maximum(peak, top)
        low = jnp.max(peak, axis=0, keepdims=True) * factor
        denom = None
        for r in range(team + 1):
            shift = low if r == team else jnp.where(gone[r], -masked_score, low)
            expo = jnp.exp2(work[r] * factor - shift)
            work[r] = expo
            part = jnp.sum(expo.reshape(rows // 8, 8, width), axis=0)
            denom = part if denom is None else denom + part
        inverse = 1.0 / jnp.sum(denom, axis=0, keepdims=True)
        for r in range(team + 1):
            probs = work[r] * inverse
            work[r] = probs
            pbuf[b, r * rows : (r + 1) * rows] = probs.astype(jnp.bfloat16)
        out_t = contract(kvt[HEAD_DIM:, cols], pbuf[b], ((1,), (0,)))
        att[b] = unstack(out_t.T).astype(jnp.bfloat16)
        ship(0, b)
        delta = jnp.sum(g2t.astype(jnp.float32) * out_t, axis=0, keepdims=True)
        for r in range(team + 1):
            grad_probs = contract(kv[b + r, :, HEAD_DIM:], g2t, ((1,), (0,)))
            dbuf[b, r * rows : (r + 1) * rows] = (work[r] * (grad_probs - delta)).astype(jnp.bfloat16)
        dq_t = contract(kvt[:HEAD_DIM, cols], dbuf[b], ((1,), (0,))) * scale
        gq[b] = unstack(dq_t.T).astype(jnp.bfloat16)
        ship(1, b)

    def back_copy(slot):
        return pltpu.make_async_remote_copy(
            src_ref=back.at[slot], dst_ref=later.at[slot],
            send_sem=back_send.at[slot], recv_sem=back_recv.at[slot],
            device_id=place(me - team), device_id_type=MESH,
        )

    def sums(slot):
        at = pl.ds(pl.multiple_of(slot * rows, rows), rows)
        return jnp.concatenate([dk[at, :] * scale, dv[at, :]], axis=1)

    @pl.loop(0, team)
    def _(b):
        at = pl.ds(pl.multiple_of(b * rows, rows), span)
        dk[at, :] += contract(dbuf[b], stack(qb[b]), ((1,), (0,)))
        dv[at, :] += contract(pbuf[b], stack(gb[b]), ((1,), (0,)))

        @pl.when(has_prev)
        def _():
            back[b] = sums(b).astype(jnp.bfloat16)
            back_copy(b).start()

    def fin_copy(to):
        return pltpu.make_async_remote_copy(
            src_ref=fin.at[to], dst_ref=land.at[member],
            send_sem=fin_send.at[to], recv_sem=fin_recv.at[member],
            device_id=place(base + to), device_id_type=MESH,
        )

    def fin_own():
        return pltpu.make_async_copy(fin.at[member], land.at[member], fin_recv.at[member])

    @pl.when(jnp.logical_not(has_next))
    def _():
        later[...] = jnp.zeros_like(later)

    @pl.loop(0, team)
    def _(slot):
        @pl.when(has_next)
        def _():
            pltpu.make_async_copy(back.at[slot], later.at[slot], back_recv.at[slot]).wait()

        fin[slot] = (sums(team + slot) + later[slot].astype(jnp.float32)).astype(jnp.bfloat16)

        @pl.when(slot != member)
        def _():
            fin_copy(slot).start()

        @pl.when(slot == member)
        def _():
            fin_own().start()

    for step in range(team):
        source = lax.rem(member + team - step, team)
        pltpu.make_async_copy(fin.at[source], land.at[source], fin_recv.at[source]).wait()
        gk = pltpu.make_async_copy(
            land.at[source, :, k_half], gk_hbm.at[:, narrow(source)], store_sem.at[0, source]
        )
        gv = pltpu.make_async_copy(
            land.at[source, :, v_half], gv_hbm.at[:, narrow(source)], store_sem.at[1, source]
        )
        gk.start()
        gv.start()

    for step in range(team):
        source = peer(step)
        for kind in range(2):
            buf, ref = ((att, att_hbm), (gq, gq_hbm))[kind]
            pltpu.make_async_copy(
                buf.at[source], ref.at[:, wide(source)], out_recv.at[kind, source]
            ).wait()
        pltpu.make_async_copy(
            land.at[source, :, k_half], gk_hbm.at[:, narrow(source)], store_sem.at[0, source]
        ).wait()
        pltpu.make_async_copy(
            land.at[source, :, v_half], gv_hbm.at[:, narrow(source)], store_sem.at[1, source]
        ).wait()
    for step in range(1, team):
        to = peer(step)
        for kind in range(4):
            in_copy(kind, to).wait_send()
        for kind in range(2):
            out_copy(kind, to).wait_send()
        fin_copy(to).wait_send()

    @pl.when(has_next)
    def _():
        for slot in range(team):
            fwd_copy(slot).wait_send()

    @pl.when(has_prev)
    def _():
        for slot in range(team):
            back_copy(slot).wait_send()


def local(tensor_size, total, queries, key_rows, value_rows, out_grad):
    rows = queries.shape[0]
    team = WINDOW // rows
    repeat = queries.shape[1] // key_rows.shape[1]
    width = repeat * HEAD_DIM
    assert key_rows.shape[1] == team * HEAD_DIM
    bf16, f32 = jnp.bfloat16, jnp.float32
    queries, key_rows, value_rows, out_grad = (
        pltpu.with_memory_space_constraint(a, pltpu.HBM)
        for a in (queries, key_rows, value_rows, out_grad)
    )
    dma = pltpu.SemaphoreType.DMA
    pairs = team * (team + 1) * rows * rows * repeat
    return pl.pallas_call(
        functools.partial(kernel, team, repeat, tensor_size, total),
        out_shape=tuple(
            jax.ShapeDtypeStruct(a.shape, bf16) for a in (queries, queries, key_rows, value_rows)
        ),
        in_specs=[pl.BlockSpec(memory_space=pl.ANY)] * 4,
        out_specs=(pl.BlockSpec(memory_space=pl.ANY),) * 4,
        scratch_shapes=[
            pltpu.VMEM((team, rows, width), bf16),
            pltpu.VMEM((team, rows, width), bf16),
            pltpu.VMEM((2 * team, rows, 2 * HEAD_DIM), bf16),
            pltpu.VMEM((2 * HEAD_DIM, 2 * team * rows), bf16),
            pltpu.VMEM((2 * team * rows, HEAD_DIM), f32),
            pltpu.VMEM((2 * team * rows, HEAD_DIM), f32),
            pltpu.VMEM((team, rows, width), bf16),
            pltpu.VMEM((team, rows, width), bf16),
            pltpu.VMEM((team, rows, 2 * HEAD_DIM), bf16),
            pltpu.VMEM((team, rows, 2 * HEAD_DIM), bf16),
            pltpu.VMEM((team, rows, 2 * HEAD_DIM), bf16),
            pltpu.VMEM((team, rows, 2 * HEAD_DIM), bf16),
            pltpu.VMEM((team + 1, rows, width), f32),
            pltpu.VMEM((team, (team + 1) * rows, width), bf16),
            pltpu.VMEM((team, (team + 1) * rows, width), bf16),
            dma((4, team)), dma((4, team)),
            dma((team,)), dma((team,)),
            dma((2, team)), dma((2, team)),
            dma((team,)), dma((team,)),
            dma((team,)), dma((team,)),
            dma((2, team)),
        ],
        compiler_params=pltpu.CompilerParams(
            collective_id=0, has_side_effects=True, vmem_limit_bytes=48 * 1024 * 1024
        ),
        cost_estimate=pl.CostEstimate(
            flops=12 * pairs * HEAD_DIM, bytes_accessed=12 * queries.size, transcendentals=pairs
        ),
    )(queries, key_rows, value_rows, out_grad)


def solution(mesh):
    spec = P(("dp", "tensor"), None)
    tensor_size = mesh.shape["tensor"]
    total = mesh.shape["dp"] * tensor_size
    return jax.shard_map(
        functools.partial(local, tensor_size, total),
        mesh=mesh, in_specs=(spec,) * 4, out_specs=(spec,) * 4, check_vma=False,
    )
```

```python
import functools

import jax
import jax.numpy as jnp
from jax import lax
from jax.experimental import pallas as pl
from jax.experimental.pallas import tpu as pltpu
from jax.sharding import PartitionSpec as P

HEAD_DIM = 128
WINDOW = 1024
QUERY_SCALE = 168
LOG2E = 1.4426950408889634

masked_score = -1e30
MESH = pl.DeviceIdType.MESH


def contract(left, right, dims):
    return lax.dot_general(left, right, (dims, ((), ())), preferred_element_type=jnp.float32)


def kernel(
    team, repeat, tensor_size, total,
    q_hbm, k_hbm, v_hbm, g_hbm,
    att_hbm, gq_hbm, gk_hbm, gv_hbm,
    qb, gb, kv, kvt, dk, dv, att, gq, back, later, fin, work, pbuf, dbuf,
    in_send, in_recv, fwd_send, fwd_recv, out_send, out_recv,
    back_send, back_recv, fin_send, fin_recv,
):
    rows = q_hbm.shape[0]
    width = repeat * HEAD_DIM
    scale = QUERY_SCALE ** (-0.5)
    me = lax.axis_index("dp") * tensor_size + lax.axis_index("tensor")
    member = lax.rem(me, team)
    base = me - member
    has_prev = me >= team
    has_next = me + team < total

    def place(index):
        return (lax.div(index, tensor_size), lax.rem(index, tensor_size))

    def peer(step):
        return lax.rem(member + step, team)

    barrier = pltpu.get_barrier_semaphore()
    for step in range(1, team):
        pl.semaphore_signal(barrier, inc=1, device_id=place(base + peer(step)), device_id_type=MESH)

    @pl.when(has_prev)
    def _():
        pl.semaphore_signal(barrier, inc=1, device_id=place(me - team), device_id_type=MESH)

    @pl.when(has_next)
    def _():
        pl.semaphore_signal(barrier, inc=1, device_id=place(me + team), device_id_type=MESH)

    pl.semaphore_wait(barrier, team - 1 + has_prev.astype(jnp.int32) + has_next.astype(jnp.int32))

    def wide(index):
        return pl.ds(pl.multiple_of(index * width, width), width)

    def narrow(index):
        return pl.ds(pl.multiple_of(index * HEAD_DIM, HEAD_DIM), HEAD_DIM)

    k_half = pl.ds(0, HEAD_DIM)
    v_half = pl.ds(HEAD_DIM, HEAD_DIM)

    def pieces(to, slot):
        return (
            (k_hbm.at[:, narrow(to)], kv.at[team + slot, :, k_half]),
            (v_hbm.at[:, narrow(to)], kv.at[team + slot, :, v_half]),
            (q_hbm.at[:, wide(to)], qb.at[slot]),
            (g_hbm.at[:, wide(to)], gb.at[slot]),
        )

    def in_copy(kind, to):
        src, dst = pieces(to, member)[kind]
        return pltpu.make_async_remote_copy(
            src_ref=src, dst_ref=dst,
            send_sem=in_send.at[kind, to], recv_sem=in_recv.at[kind, member],
            device_id=place(base + to), device_id_type=MESH,
        )

    def in_wait(kind, source):
        src, dst = pieces(member, source)[kind]
        pltpu.make_async_copy(src, dst, in_recv.at[kind, source]).wait()

    for kind in range(4):
        src, dst = pieces(member, member)[kind]
        pltpu.make_async_copy(src, dst, in_recv.at[kind, member]).start()
    for kinds in ((0, 1), (2, 3)):
        for step in range(1, team):
            for kind in kinds:
                in_copy(kind, peer(step)).start()

    dk[...] = jnp.zeros_like(dk)
    dv[...] = jnp.zeros_like(dv)

    def fwd_copy(slot):
        return pltpu.make_async_remote_copy(
            src_ref=kv.at[team + slot], dst_ref=kv.at[slot],
            send_sem=fwd_send.at[slot], recv_sem=fwd_recv.at[slot],
            device_id=place(me + team), device_id_type=MESH,
        )

    for step in range(team):
        source = peer(step)
        in_wait(0, source)
        in_wait(1, source)

        @pl.when(has_next)
        def _():
            fwd_copy(source).start()

    def turn(slot):
        kvt[:, pl.ds(pl.multiple_of(slot * rows, rows), rows)] = kv[slot].T

    @pl.loop(0, team)
    def _(slot):
        turn(team + slot)

    @pl.when(jnp.logical_not(has_prev))
    def _():
        kv[pl.ds(0, team)] = jnp.zeros((team,) + kv.shape[1:], kv.dtype)

    @pl.loop(0, team)
    def _(step):
        slot = peer(step)

        @pl.when(has_prev)
        def _():
            pltpu.make_async_copy(kv.at[team + slot], kv.at[slot], fwd_recv.at[slot]).wait()

        turn(slot)

    span = (team + 1) * rows
    key_at = lax.broadcasted_iota(jnp.int32, (rows, repeat * rows), 0)
    query_at = lax.rem(lax.broadcasted_iota(jnp.int32, (rows, repeat * rows), 1), rows)
    factor = scale * LOG2E

    def stack(block):
        return jnp.concatenate(
            [block[:, h * HEAD_DIM : (h + 1) * HEAD_DIM] for h in range(repeat)], axis=0
        )

    def unstack(block):
        return jnp.concatenate([block[h * rows : (h + 1) * rows] for h in range(repeat)], axis=1)

    def out_copy(kind, to):
        buf, ref = ((att, att_hbm), (gq, gq_hbm))[kind]
        return pltpu.make_async_remote_copy(
            src_ref=buf.at[to], dst_ref=ref.at[:, wide(member)],
            send_sem=out_send.at[kind, to], recv_sem=out_recv.at[kind, member],
            device_id=place(base + to), device_id_type=MESH,
        )

    def out_own(kind):
        buf, ref = ((att, att_hbm), (gq, gq_hbm))[kind]
        return pltpu.make_async_copy(
            buf.at[member], ref.at[:, wide(member)], out_recv.at[kind, member]
        )

    def ship(kind, to):
        @pl.when(to != member)
        def _():
            out_copy(kind, to).start()

        @pl.when(to == member)
        def _():
            out_own(kind).start()

    lanes = 4

    @pl.loop(0, team // lanes)
    def _(turn_at):
        blocks = [peer(turn_at * lanes + u) for u in range(lanes)]
        for b in blocks:
            in_wait(2, b)
            in_wait(3, b)
        q2t = [stack(qb[b]).T for b in blocks]
        g2t = [stack(gb[b]).T for b in blocks]
        cols = [pl.ds(pl.multiple_of(b * rows, rows), span) for b in blocks]
        lows = []
        for u, b in enumerate(blocks):
            peak = None
            for r in range(team + 1):
                part = contract(kv[b + r, :, :HEAD_DIM], q2t[u], ((1,), (0,)))
                if r == 0:
                    part = jnp.where(key_at > query_at, part, masked_score)
                if r == team:
                    part = jnp.where(key_at <= query_at, part, masked_score)
                work[u, r] = part
                top = jnp.max(part.reshape(rows // 8, 8, width), axis=0)
                if r < team:
                    gone = jnp.logical_and(jnp.logical_not(has_prev), b + r < team)
                    top = jnp.where(gone, masked_score, top)
                peak = top if peak is None else jnp.maximum(peak, top)
            lows.append(jnp.max(peak, axis=0, keepdims=True) * factor)
        outs = []
        for u, b in enumerate(blocks):
            denom = None
            for r in range(team + 1):
                shift = lows[u]
                if r < team:
                    gone = jnp.logical_and(jnp.logical_not(has_prev), b + r < team)
                    shift = jnp.where(gone, -masked_score, shift)
                expo = jnp.exp2(work[u, r] * factor - shift)
                work[u, r] = expo
                part = jnp.sum(expo.reshape(rows // 8, 8, width), axis=0)
                denom = part if denom is None else denom + part
            inverse = 1.0 / jnp.sum(denom, axis=0, keepdims=True)
            for r in range(team + 1):
                probs = work[u, r] * inverse
                work[u, r] = probs
                pbuf[b, r * rows : (r + 1) * rows] = probs.astype(jnp.bfloat16)
            outs.append(contract(kvt[HEAD_DIM:, cols[u]], pbuf[b], ((1,), (0,))))
        for u, b in enumerate(blocks):
            out_t = outs[u]
            att[b] = unstack(out_t.T).astype(jnp.bfloat16)
            delta = jnp.sum(g2t[u].astype(jnp.float32) * out_t, axis=0, keepdims=True)
            for r in range(team + 1):
                grad_probs = contract(kv[b + r, :, HEAD_DIM:], g2t[u], ((1,), (0,)))
                dbuf[b, r * rows : (r + 1) * rows] = (
                    work[u, r] * (grad_probs - delta)
                ).astype(jnp.bfloat16)
            dq_t = contract(kvt[:HEAD_DIM, cols[u]], dbuf[b], ((1,), (0,))) * scale
            gq[b] = unstack(dq_t.T).astype(jnp.bfloat16)
        for b in blocks:
            ship(0, b)
            ship(1, b)

    def back_copy(slot):
        return pltpu.make_async_remote_copy(
            src_ref=back.at[slot], dst_ref=later.at[slot],
            send_sem=back_send.at[slot], recv_sem=back_recv.at[slot],
            device_id=place(me - team), device_id_type=MESH,
        )

    def sums(slot):
        at = pl.ds(pl.multiple_of(slot * rows, rows), rows)
        return jnp.concatenate([dk[at, :] * scale, dv[at, :]], axis=1)

    @pl.loop(0, team)
    def _(b):
        at = pl.ds(pl.multiple_of(b * rows, rows), span)
        dk[at, :] += contract(dbuf[b], stack(qb[b]), ((1,), (0,)))
        dv[at, :] += contract(pbuf[b], stack(gb[b]), ((1,), (0,)))

        @pl.when(has_prev)
        def _():
            back[b] = sums(b).astype(jnp.bfloat16)
            back_copy(b).start()

    def fin_refs(kind, slot, source):
        half, ref = ((k_half, gk_hbm), (v_half, gv_hbm))[kind]
        return fin.at[slot, :, half], ref.at[:, narrow(source)]

    def fin_copy(kind, to):
        src, dst = fin_refs(kind, to, member)
        return pltpu.make_async_remote_copy(
            src_ref=src, dst_ref=dst,
            send_sem=fin_send.at[kind, to], recv_sem=fin_recv.at[kind, member],
            device_id=place(base + to), device_id_type=MESH,
        )

    def fin_local(kind, slot):
        src, dst = fin_refs(kind, slot, slot)
        return pltpu.make_async_copy(src, dst, fin_recv.at[kind, slot])

    @pl.when(jnp.logical_not(has_next))
    def _():
        later[...] = jnp.zeros_like(later)

    @pl.loop(0, team)
    def _(slot):
        @pl.when(has_next)
        def _():
            pltpu.make_async_copy(back.at[slot], later.at[slot], back_recv.at[slot]).wait()

        fin[slot] = (sums(team + slot) + later[slot].astype(jnp.float32)).astype(jnp.bfloat16)

        @pl.when(slot != member)
        def _():
            fin_copy(0, slot).start()
            fin_copy(1, slot).start()

        @pl.when(slot == member)
        def _():
            fin_local(0, slot).start()
            fin_local(1, slot).start()

    for step in range(team):
        source = peer(step)
        for kind in range(2):
            buf, ref = ((att, att_hbm), (gq, gq_hbm))[kind]
            pltpu.make_async_copy(
                buf.at[source], ref.at[:, wide(source)], out_recv.at[kind, source]
            ).wait()
        for kind in range(2):
            fin_local(kind, source).wait()
    for step in range(1, team):
        to = peer(step)
        for kind in range(4):
            in_copy(kind, to).wait_send()
        for kind in range(2):
            out_copy(kind, to).wait_send()
        for kind in range(2):
            fin_copy(kind, to).wait_send()

    @pl.when(has_next)
    def _():
        for slot in range(team):
            fwd_copy(slot).wait_send()

    @pl.when(has_prev)
    def _():
        for slot in range(team):
            back_copy(slot).wait_send()


def local(tensor_size, total, queries, key_rows, value_rows, out_grad):
    rows = queries.shape[0]
    team = WINDOW // rows
    repeat = queries.shape[1] // key_rows.shape[1]
    width = repeat * HEAD_DIM
    assert key_rows.shape[1] == team * HEAD_DIM
    bf16, f32 = jnp.bfloat16, jnp.float32
    queries, key_rows, value_rows, out_grad = (
        pltpu.with_memory_space_constraint(a, pltpu.HBM)
        for a in (queries, key_rows, value_rows, out_grad)
    )
    dma = pltpu.SemaphoreType.DMA
    pairs = team * (team + 1) * rows * rows * repeat
    return pl.pallas_call(
        functools.partial(kernel, team, repeat, tensor_size, total),
        out_shape=tuple(
            jax.ShapeDtypeStruct(a.shape, bf16) for a in (queries, queries, key_rows, value_rows)
        ),
        in_specs=[pl.BlockSpec(memory_space=pl.ANY)] * 4,
        out_specs=(pl.BlockSpec(memory_space=pl.ANY),) * 4,
        scratch_shapes=[
            pltpu.VMEM((team, rows, width), bf16),
            pltpu.VMEM((team, rows, width), bf16),
            pltpu.VMEM((2 * team, rows, 2 * HEAD_DIM), bf16),
            pltpu.VMEM((2 * HEAD_DIM, 2 * team * rows), bf16),
            pltpu.VMEM((2 * team * rows, HEAD_DIM), f32),
            pltpu.VMEM((2 * team * rows, HEAD_DIM), f32),
            pltpu.VMEM((team, rows, width), bf16),
            pltpu.VMEM((team, rows, width), bf16),
            pltpu.VMEM((team, rows, 2 * HEAD_DIM), bf16),
            pltpu.VMEM((team, rows, 2 * HEAD_DIM), bf16),
            pltpu.VMEM((team, rows, 2 * HEAD_DIM), bf16),
            pltpu.VMEM((4, team + 1, rows, width), f32),
            pltpu.VMEM((team, (team + 1) * rows, width), bf16),
            pltpu.VMEM((team, (team + 1) * rows, width), bf16),
            dma((4, team)), dma((4, team)),
            dma((team,)), dma((team,)),
            dma((2, team)), dma((2, team)),
            dma((team,)), dma((team,)),
            dma((2, team)), dma((2, team)),
        ],
        compiler_params=pltpu.CompilerParams(
            collective_id=0, has_side_effects=True, vmem_limit_bytes=48 * 1024 * 1024
        ),
        cost_estimate=pl.CostEstimate(
            flops=12 * pairs * HEAD_DIM, bytes_accessed=12 * queries.size, transcendentals=pairs
        ),
    )(queries, key_rows, value_rows, out_grad)


def solution(mesh):
    spec = P(("dp", "tensor"), None)
    tensor_size = mesh.shape["tensor"]
    total = mesh.shape["dp"] * tensor_size
    return jax.shard_map(
        functools.partial(local, tensor_size, total),
        mesh=mesh, in_specs=(spec,) * 4, out_specs=(spec,) * 4, check_vma=False,
    )
```

```python
import functools

import jax
import jax.numpy as jnp
from jax import lax
from jax.experimental import pallas as pl
from jax.experimental.pallas import tpu as pltpu
from jax.sharding import PartitionSpec as P

HEAD_DIM = 128
WINDOW = 1024
QUERY_SCALE = 168
LOG2E = 1.4426950408889634

masked_score = -1e30
MESH = pl.DeviceIdType.MESH


def contract(left, right, dims):
    return lax.dot_general(left, right, (dims, ((), ())), preferred_element_type=jnp.float32)


def kernel(
    team, repeat, tensor_size, total,
    q_hbm, k_hbm, v_hbm, g_hbm,
    att_hbm, gq_hbm, gk_hbm, gv_hbm,
    qb, gb, kv, kvt, dk, dv, att, gq, back, later, fin, work, pbuf, dbuf,
    in_send, in_recv, fwd_send, fwd_recv, out_send, out_recv,
    back_send, back_recv, fin_send, fin_recv,
):
    rows = q_hbm.shape[0]
    width = repeat * HEAD_DIM
    scale = QUERY_SCALE ** (-0.5)
    me = lax.axis_index("dp") * tensor_size + lax.axis_index("tensor")
    member = lax.rem(me, team)
    base = me - member
    has_prev = me >= team
    has_next = me + team < total

    def place(index):
        return (lax.div(index, tensor_size), lax.rem(index, tensor_size))

    def peer(step):
        return lax.rem(member + step, team)

    def giver(step):
        return lax.rem(member + team - step, team)

    barrier = pltpu.get_barrier_semaphore()
    for step in range(1, team):
        pl.semaphore_signal(barrier, inc=1, device_id=place(base + peer(step)), device_id_type=MESH)

    @pl.when(has_prev)
    def _():
        pl.semaphore_signal(barrier, inc=1, device_id=place(me - team), device_id_type=MESH)

    @pl.when(has_next)
    def _():
        pl.semaphore_signal(barrier, inc=1, device_id=place(me + team), device_id_type=MESH)

    pl.semaphore_wait(barrier, team - 1 + has_prev.astype(jnp.int32) + has_next.astype(jnp.int32))

    def wide(index):
        return pl.ds(pl.multiple_of(index * width, width), width)

    def narrow(index):
        return pl.ds(pl.multiple_of(index * HEAD_DIM, HEAD_DIM), HEAD_DIM)

    k_half = pl.ds(0, HEAD_DIM)
    v_half = pl.ds(HEAD_DIM, HEAD_DIM)

    def pieces(to, slot):
        return (
            (k_hbm.at[:, narrow(to)], kv.at[team + slot, :, k_half]),
            (v_hbm.at[:, narrow(to)], kv.at[team + slot, :, v_half]),
            (q_hbm.at[:, wide(to)], qb.at[slot]),
            (g_hbm.at[:, wide(to)], gb.at[slot]),
        )

    def in_copy(kind, to):
        src, dst = pieces(to, member)[kind]
        return pltpu.make_async_remote_copy(
            src_ref=src, dst_ref=dst,
            send_sem=in_send.at[kind, to], recv_sem=in_recv.at[kind, member],
            device_id=place(base + to), device_id_type=MESH,
        )

    def in_wait(kind, source):
        src, dst = pieces(member, source)[kind]
        pltpu.make_async_copy(src, dst, in_recv.at[kind, source]).wait()

    for kind in range(4):
        src, dst = pieces(member, member)[kind]
        pltpu.make_async_copy(src, dst, in_recv.at[kind, member]).start()
    for kinds in ((0, 1), (2, 3)):
        for step in range(1, team):
            for kind in kinds:
                in_copy(kind, peer(step)).start()

    dk[...] = jnp.zeros_like(dk)
    dv[...] = jnp.zeros_like(dv)

    def fwd_copy(slot):
        return pltpu.make_async_remote_copy(
            src_ref=kv.at[team + slot], dst_ref=kv.at[slot],
            send_sem=fwd_send.at[slot], recv_sem=fwd_recv.at[slot],
            device_id=place(me + team), device_id_type=MESH,
        )

    for step in range(team):
        source = giver(step)
        in_wait(0, source)
        in_wait(1, source)

        @pl.when(has_next)
        def _():
            fwd_copy(source).start()

    def turn(slot):
        kvt[:, pl.ds(pl.multiple_of(slot * rows, rows), rows)] = kv[slot].T

    @pl.loop(0, team)
    def _(slot):
        turn(team + slot)

    @pl.when(jnp.logical_not(has_prev))
    def _():
        kv[pl.ds(0, team)] = jnp.zeros((team,) + kv.shape[1:], kv.dtype)

    @pl.loop(0, team)
    def _(step):
        slot = giver(step)

        @pl.when(has_prev)
        def _():
            pltpu.make_async_copy(kv.at[team + slot], kv.at[slot], fwd_recv.at[slot]).wait()

        turn(slot)

    span = (team + 1) * rows
    key_at = lax.broadcasted_iota(jnp.int32, (rows, repeat * rows), 0)
    query_at = lax.rem(lax.broadcasted_iota(jnp.int32, (rows, repeat * rows), 1), rows)
    factor = scale * LOG2E

    def stack(block):
        return jnp.concatenate(
            [block[:, h * HEAD_DIM : (h + 1) * HEAD_DIM] for h in range(repeat)], axis=0
        )

    def unstack(block):
        return jnp.concatenate([block[h * rows : (h + 1) * rows] for h in range(repeat)], axis=1)

    def out_copy(kind, to):
        buf, ref = ((att, att_hbm), (gq, gq_hbm))[kind]
        return pltpu.make_async_remote_copy(
            src_ref=buf.at[to], dst_ref=ref.at[:, wide(member)],
            send_sem=out_send.at[kind, to], recv_sem=out_recv.at[kind, member],
            device_id=place(base + to), device_id_type=MESH,
        )

    def out_own(kind):
        buf, ref = ((att, att_hbm), (gq, gq_hbm))[kind]
        return pltpu.make_async_copy(
            buf.at[member], ref.at[:, wide(member)], out_recv.at[kind, member]
        )

    def ship(kind, to):
        @pl.when(to != member)
        def _():
            out_copy(kind, to).start()

        @pl.when(to == member)
        def _():
            out_own(kind).start()

    lanes = 4

    @pl.loop(0, team // lanes)
    def _(turn_at):
        blocks = [giver(turn_at * lanes + u) for u in range(lanes)]
        for b in blocks:
            in_wait(2, b)
            in_wait(3, b)
        q2t = [stack(qb[b]).T for b in blocks]
        g2t = [stack(gb[b]).T for b in blocks]
        cols = [pl.ds(pl.multiple_of(b * rows, rows), span) for b in blocks]
        lows = []
        for u, b in enumerate(blocks):
            peak = None
            for r in range(team + 1):
                part = contract(kv[b + r, :, :HEAD_DIM], q2t[u], ((1,), (0,)))
                if r == 0:
                    part = jnp.where(key_at > query_at, part, masked_score)
                if r == team:
                    part = jnp.where(key_at <= query_at, part, masked_score)
                work[u, r] = part
                top = jnp.max(part.reshape(rows // 8, 8, width), axis=0)
                if r < team:
                    gone = jnp.logical_and(jnp.logical_not(has_prev), b + r < team)
                    top = jnp.where(gone, masked_score, top)
                peak = top if peak is None else jnp.maximum(peak, top)
            lows.append(jnp.max(peak, axis=0, keepdims=True) * factor)
        outs = []
        for u, b in enumerate(blocks):
            denom = None
            for r in range(team + 1):
                shift = lows[u]
                if r < team:
                    gone = jnp.logical_and(jnp.logical_not(has_prev), b + r < team)
                    shift = jnp.where(gone, -masked_score, shift)
                expo = jnp.exp2(work[u, r] * factor - shift)
                work[u, r] = expo
                part = jnp.sum(expo.reshape(rows // 8, 8, width), axis=0)
                denom = part if denom is None else denom + part
            inverse = 1.0 / jnp.sum(denom, axis=0, keepdims=True)
            for r in range(team + 1):
                probs = work[u, r] * inverse
                work[u, r] = probs
                pbuf[b, r * rows : (r + 1) * rows] = probs.astype(jnp.bfloat16)
            outs.append(contract(kvt[HEAD_DIM:, cols[u]], pbuf[b], ((1,), (0,))))
        for u, b in enumerate(blocks):
            out_t = outs[u]
            att[b] = unstack(out_t.T).astype(jnp.bfloat16)
            delta = jnp.sum(g2t[u].astype(jnp.float32) * out_t, axis=0, keepdims=True)
            for r in range(team + 1):
                grad_probs = contract(kv[b + r, :, HEAD_DIM:], g2t[u], ((1,), (0,)))
                dbuf[b, r * rows : (r + 1) * rows] = (
                    work[u, r] * (grad_probs - delta)
                ).astype(jnp.bfloat16)
            dq_t = contract(kvt[:HEAD_DIM, cols[u]], dbuf[b], ((1,), (0,))) * scale
            gq[b] = unstack(dq_t.T).astype(jnp.bfloat16)
        for b in blocks:
            ship(0, b)
            ship(1, b)

    def back_copy(slot):
        return pltpu.make_async_remote_copy(
            src_ref=back.at[slot], dst_ref=later.at[slot],
            send_sem=back_send.at[slot], recv_sem=back_recv.at[slot],
            device_id=place(me - team), device_id_type=MESH,
        )

    def sums(slot):
        at = pl.ds(pl.multiple_of(slot * rows, rows), rows)
        return jnp.concatenate([dk[at, :] * scale, dv[at, :]], axis=1)

    @pl.loop(0, team)
    def _(b):
        at = pl.ds(pl.multiple_of(b * rows, rows), span)
        dk[at, :] += contract(dbuf[b], stack(qb[b]), ((1,), (0,)))
        dv[at, :] += contract(pbuf[b], stack(gb[b]), ((1,), (0,)))

        @pl.when(has_prev)
        def _():
            back[b] = sums(b).astype(jnp.bfloat16)
            back_copy(b).start()

    def fin_refs(kind, slot, source):
        half, ref = ((k_half, gk_hbm), (v_half, gv_hbm))[kind]
        return fin.at[slot, :, half], ref.at[:, narrow(source)]

    def fin_copy(kind, to):
        src, dst = fin_refs(kind, to, member)
        return pltpu.make_async_remote_copy(
            src_ref=src, dst_ref=dst,
            send_sem=fin_send.at[kind, to], recv_sem=fin_recv.at[kind, member],
            device_id=place(base + to), device_id_type=MESH,
        )

    def fin_local(kind, slot):
        src, dst = fin_refs(kind, slot, slot)
        return pltpu.make_async_copy(src, dst, fin_recv.at[kind, slot])

    @pl.when(jnp.logical_not(has_next))
    def _():
        later[...] = jnp.zeros_like(later)

    @pl.loop(0, team)
    def _(slot):
        @pl.when(has_next)
        def _():
            pltpu.make_async_copy(back.at[slot], later.at[slot], back_recv.at[slot]).wait()

        fin[slot] = (sums(team + slot) + later[slot].astype(jnp.float32)).astype(jnp.bfloat16)

        @pl.when(slot != member)
        def _():
            fin_copy(0, slot).start()
            fin_copy(1, slot).start()

        @pl.when(slot == member)
        def _():
            fin_local(0, slot).start()
            fin_local(1, slot).start()

    for step in range(team):
        source = peer(step)
        for kind in range(2):
            buf, ref = ((att, att_hbm), (gq, gq_hbm))[kind]
            pltpu.make_async_copy(
                buf.at[source], ref.at[:, wide(source)], out_recv.at[kind, source]
            ).wait()
        for kind in range(2):
            fin_local(kind, source).wait()
    for step in range(1, team):
        to = peer(step)
        for kind in range(4):
            in_copy(kind, to).wait_send()
        for kind in range(2):
            out_copy(kind, to).wait_send()
        for kind in range(2):
            fin_copy(kind, to).wait_send()

    @pl.when(has_next)
    def _():
        for slot in range(team):
            fwd_copy(slot).wait_send()

    @pl.when(has_prev)
    def _():
        for slot in range(team):
            back_copy(slot).wait_send()


def local(tensor_size, total, queries, key_rows, value_rows, out_grad):
    rows = queries.shape[0]
    team = WINDOW // rows
    repeat = queries.shape[1] // key_rows.shape[1]
    width = repeat * HEAD_DIM
    assert key_rows.shape[1] == team * HEAD_DIM
    bf16, f32 = jnp.bfloat16, jnp.float32
    queries, key_rows, value_rows, out_grad = (
        pltpu.with_memory_space_constraint(a, pltpu.HBM)
        for a in (queries, key_rows, value_rows, out_grad)
    )
    dma = pltpu.SemaphoreType.DMA
    pairs = team * (team + 1) * rows * rows * repeat
    return pl.pallas_call(
        functools.partial(kernel, team, repeat, tensor_size, total),
        out_shape=tuple(
            jax.ShapeDtypeStruct(a.shape, bf16) for a in (queries, queries, key_rows, value_rows)
        ),
        in_specs=[pl.BlockSpec(memory_space=pl.ANY)] * 4,
        out_specs=(pl.BlockSpec(memory_space=pl.ANY),) * 4,
        scratch_shapes=[
            pltpu.VMEM((team, rows, width), bf16),
            pltpu.VMEM((team, rows, width), bf16),
            pltpu.VMEM((2 * team, rows, 2 * HEAD_DIM), bf16),
            pltpu.VMEM((2 * HEAD_DIM, 2 * team * rows), bf16),
            pltpu.VMEM((2 * team * rows, HEAD_DIM), f32),
            pltpu.VMEM((2 * team * rows, HEAD_DIM), f32),
            pltpu.VMEM((team, rows, width), bf16),
            pltpu.VMEM((team, rows, width), bf16),
            pltpu.VMEM((team, rows, 2 * HEAD_DIM), bf16),
            pltpu.VMEM((team, rows, 2 * HEAD_DIM), bf16),
            pltpu.VMEM((team, rows, 2 * HEAD_DIM), bf16),
            pltpu.VMEM((4, team + 1, rows, width), f32),
            pltpu.VMEM((team, (team + 1) * rows, width), bf16),
            pltpu.VMEM((team, (team + 1) * rows, width), bf16),
            dma((4, team)), dma((4, team)),
            dma((team,)), dma((team,)),
            dma((2, team)), dma((2, team)),
            dma((team,)), dma((team,)),
            dma((2, team)), dma((2, team)),
        ],
        compiler_params=pltpu.CompilerParams(
            collective_id=0, has_side_effects=True, vmem_limit_bytes=48 * 1024 * 1024
        ),
        cost_estimate=pl.CostEstimate(
            flops=12 * pairs * HEAD_DIM, bytes_accessed=12 * queries.size, transcendentals=pairs
        ),
    )(queries, key_rows, value_rows, out_grad)


def solution(mesh):
    spec = P(("dp", "tensor"), None)
    tensor_size = mesh.shape["tensor"]
    total = mesh.shape["dp"] * tensor_size
    return jax.shard_map(
        functools.partial(local, tensor_size, total),
        mesh=mesh, in_specs=(spec,) * 4, out_specs=(spec,) * 4, check_vma=False,
    )
```
